32 devices in a mesh: pipe: 2 (over y), ctx: 8 (over z, x), tp: 2 (over core).
Axes of the slice: x: 2, y: 2, z: 4, core: 2. Of those that a mesh axis runs over, the one named last changes fastest.
Arguments:
- stream: bfloat16 [2, 1024, 4096], P('pipe', 'ctx', 'tp'), may hold values from -6 to 6
- queries: bfloat16 [2, 1024, 4096], P('pipe', 'ctx', 'tp'), may hold values from -5 to 5
- keys: bfloat16 [2, 1024, 1024], P('pipe', 'ctx', 'tp'), may hold values from -5 to 5
- values: bfloat16 [2, 1024, 1024], P('pipe', 'ctx', 'tp'), may hold values from -6 to 6
- segments: int32 [2, 1024], P('pipe', 'ctx'), may hold values from 0 to 5, never falling along the last dimension, each value on 1 to 512 neighbouring positions
- norm_gain: bfloat16 [4096], P('tp'), may hold values from 0.25 to 1.75
Outputs:
- arrived: bfloat16 [2, 1024, 4096], P('pipe', 'ctx', 'tp')
- normed: bfloat16 [2, 1024, 4096], P('pipe', 'ctx', 'tp')
The draws below stay inside these ranges and needn't reach their ends.
Inputs may be any that keep to these rules, and one draw needn't show every extreme that they name: `segments`: in each section's micro-batch the document number never falls along positions; each document holds 1 to half of 1024 positions, and one holds exactly half of 1024.
All inputs are finite; a program needn't handle non-finite values.
Results may differ from the reference program's by a relative error of at most 0.006.
Values may be sent and summed in bfloat16 or wider, within the bound.
No kernel may reach another device: no remote copies, remote signals or barrier semaphores. Data moves between devices by JAX's collectives and lax.ppermute only.
A program may use at most 128 MiB of HBM per device.

```python
import math
import jax
import jax.numpy as jnp
import numpy as np
from jax import lax

QUERY_HEADS = 32
KEY_VALUE_HEADS = 8
HEAD_SIZE = 128
DOCS = 6
TOK_DEV = 128
RELAY_SECTIONS = 2
MICRO_POSITIONS = 1024
N_CTX = 8


def unsigned_entries(key, width):
    return jax.random.truncated_normal(key, -5.0, 5.0, (RELAY_SECTIONS, MICRO_POSITIONS, width), jnp.float32)


def draw_queries(key, part):
    table_entries = unsigned_entries(jax.random.fold_in(key, 11), QUERY_HEADS * HEAD_SIZE)
    return table_entries.astype(jnp.bfloat16)


def draw_keys(key, part):
    table_entries = unsigned_entries(jax.random.fold_in(key, 13), KEY_VALUE_HEADS * HEAD_SIZE)
    return table_entries.astype(jnp.bfloat16)


def level_of(own_key, extent, shards, smallest, largest):
    factor_of, own = 1.0, jax.random.fold_in(own_key, 6)
    for axis_at, parts in shards:
        steps = jnp.exp(jax.random.uniform(jax.random.fold_in(own, axis_at), (parts,), jnp.float32, smallest / len(shards), largest / len(shards)))
        factor_of = factor_of * jnp.repeat(steps, extent[axis_at] // parts).reshape([-1 if axis == axis_at else 1 for axis in range(len(extent))])
    return factor_of


def length_profile(amount, total, limit, slope):
    loads = [(1 << 20) // math.isqrt(rank ** slope) + 1 for rank in range(2, amount + 1)]
    rest, given = total - limit - (amount - 1), [1] * (amount - 1)
    while rest > 0:
        candidates = [i for i in range(amount - 1) if given[i] < limit]
        mass, left = sum([loads[i] for i in candidates]), rest
        for i in candidates:
            extra = min(limit - given[i], max(1, left * loads[i] // mass), rest)
            given[i] = given[i] + extra
            rest = rest - extra
    return np.array([limit] + given)


def uneven_parts(stream_key, number_of, total, bound, slope):
    if number_of == 2:
        one = jax.random.randint(stream_key, (), max(1, total - bound), min(bound, total - 1) + 1)
        return jnp.stack([one, total - one])
    sizes = jnp.asarray(length_profile(number_of, total, bound, slope), jnp.int32)
    couples = (number_of - 1) // 2
    giver, receiver = sizes[1:1 + 2 * couples:2], sizes[2:2 + 2 * couples:2]
    room = jnp.minimum(giver - 1, bound - receiver)
    shifted = jax.random.randint(jax.random.fold_in(stream_key, 1), (couples,), 0, 1 << 20) % (room + 1)
    sizes = sizes.at[1:1 + 2 * couples:2].set(giver - shifted).at[2:2 + 2 * couples:2].set(receiver + shifted)
    return sizes[jax.random.permutation(jax.random.fold_in(stream_key, 2), number_of)]


def centred(stream_key, dims, scale, limit, cuts=(), kind=jnp.bfloat16):
    loudness = level_of(stream_key, dims, cuts, -0.22, 0.18) if cuts else 1.0
    values = jax.random.normal(stream_key, dims, jnp.float32) * scale * loudness
    return jnp.minimum(jnp.maximum(values, -limit), limit).astype(kind)


def setup_inputs(seed: int = 0) -> dict:
    splits = jax.random.split(jax.random.key(seed), 7)
    return {
        "stream": centred(splits[0], (RELAY_SECTIONS, MICRO_POSITIONS, QUERY_HEADS * HEAD_SIZE), 1.0, 6.0, ((0, 2), (1, 8), (2, 2))),
        "queries": draw_queries(jax.random.fold_in(splits[6], 71), 0),
        "keys": draw_keys(jax.random.fold_in(splits[6], 71), 0),
        "values": centred(splits[3], (RELAY_SECTIONS, MICRO_POSITIONS, KEY_VALUE_HEADS * HEAD_SIZE), 1.0, 6.0, ((0, 2), (1, 8), (2, 2))),
        "segments": jax.vmap(lambda own: jnp.searchsorted(jnp.cumsum(uneven_parts(own, DOCS, MICRO_POSITIONS, TOK_DEV * N_CTX // 2, 2)), jnp.arange(MICRO_POSITIONS), side="right"))(jax.random.split(splits[4], RELAY_SECTIONS)).reshape((RELAY_SECTIONS, MICRO_POSITIONS)).astype(jnp.int32),
        "norm_gain": jnp.clip(1.0 + 0.15 * jax.random.normal(splits[5], (QUERY_HEADS * HEAD_SIZE,), jnp.float32), 0.25, 1.75).astype(jnp.bfloat16),
    }


def attend_section(query_row_block, key_row_block, value_row_block, seg_ids):
    span_length = query_row_block.shape[0]
    query_group_size = QUERY_HEADS // KEY_VALUE_HEADS
    span = math.gcd(span_length, 512)
    score_scale = HEAD_SIZE ** (-0.5)
    positions = jnp.arange(span_length, dtype=jnp.int32)
    query_head_stack = query_row_block.reshape(span_length, KEY_VALUE_HEADS, query_group_size, HEAD_SIZE).transpose(1, 2, 0, 3)
    key_head_stack = key_row_block.reshape(span_length, KEY_VALUE_HEADS, HEAD_SIZE).transpose(1, 0, 2)
    value_head_stack = value_row_block.reshape(span_length, KEY_VALUE_HEADS, HEAD_SIZE).transpose(1, 0, 2)

    def per_head(operands):
        query_head, key_head, value_head = operands
        key_wide = key_head.astype(jnp.float32)
        value_wide = value_head.astype(jnp.float32)

        def per_block(row_start):
            query_block = lax.dynamic_slice_in_dim(query_head, row_start, span, 1).astype(jnp.float32)
            query_pos = row_start + jnp.arange(span, dtype=jnp.int32)
            query_seg = lax.dynamic_slice_in_dim(seg_ids, row_start, span, 0)
            scores = jnp.einsum('gqd,kd->gqk', query_block, key_wide) * score_scale
            allowed = (positions[None, :] <= query_pos[:, None]) & (seg_ids[None, :] == query_seg[:, None])
            scores = jnp.where(allowed[None], scores, -jnp.inf)
            top = lax.optimization_barrier(jnp.max(scores, axis=-1, keepdims=True))
            weights = jnp.where(allowed[None], jnp.exp(scores - top), 0.0)
            total = lax.optimization_barrier(jnp.sum(weights, axis=-1, keepdims=True))
            rounded = lax.optimization_barrier(weights.astype(jnp.bfloat16)).astype(jnp.float32)
            mixed = jnp.einsum('gqk,kd->gqd', rounded, value_wide) / total
            return mixed.astype(jnp.bfloat16)
        starts = jnp.arange(0, span_length, span, dtype=jnp.int32)
        blocks = lax.map(per_block, starts)
        return blocks.transpose(1, 0, 2, 3).reshape(query_group_size, span_length, HEAD_SIZE)
    heads_out = lax.map(per_head, (query_head_stack, key_head_stack, value_head_stack))
    return heads_out.transpose(2, 0, 1, 3).reshape(span_length, QUERY_HEADS * HEAD_SIZE)

def reference(stream, queries, keys, values, segments, norm_gain):
    advanced_list = []
    for section in range(stream.shape[0]):
        attended = attend_section(queries[section], keys[section], values[section], segments[section])
        attended = lax.optimization_barrier(attended).astype(jnp.float32)
        advanced_list.append((stream[section].astype(jnp.float32) + attended).astype(jnp.bfloat16))
    advanced = jnp.stack(advanced_list)
    arrived = jnp.roll(advanced, 1, axis=0)
    wide = arrived.astype(jnp.float32)
    mean_square = lax.optimization_barrier(jnp.mean(wide * wide, axis=-1, keepdims=True))
    normed = (wide * lax.rsqrt(mean_square + 1e-05) * norm_gain.astype(jnp.float32)).astype(jnp.bfloat16)
    return (arrived, normed)
```

```python
import functools
import math

import jax
import jax.numpy as jnp
from jax import lax
from jax.experimental import pallas as pl
from jax.experimental.pallas import tpu as pltpu
from jax.sharding import PartitionSpec as P

HEAD = 128
FEATURES = 4096
EPS = 1e-05
SEG_ROWS = 16
NEG = -1e30
VMEM_LIMIT = 40 * 1024 * 1024


def route(x, axes, move):
    sizes = [lax.axis_size(a) for a in axes]
    pairs = []
    for src in range(math.prod(sizes)):
        at, rest = [], src
        for s in reversed(sizes):
            at.insert(0, rest % s)
            rest //= s
        to = 0
        for s, v in zip(sizes, move(*at)):
            to = to * s + v
        pairs.append((src, to))
    return lax.ppermute(x, tuple(axes) if len(axes) > 1 else axes[0], pairs)


def turned(row):
    return jnp.transpose(jnp.broadcast_to(row, (HEAD, HEAD)))


def pack_kernel(halves, k_ref, v_ref, seg_ref, keep_ref, send_ref):
    side = lax.axis_index("ctx") % 2
    seg = jnp.broadcast_to(seg_ref[...], (SEG_ROWS, HEAD)).astype(jnp.float32).astype(jnp.bfloat16)
    for out, half in ((keep_ref, side), (send_ref, 1 - side)):
        for h in range(halves):
            at = pl.ds(pl.multiple_of((half * halves + h) * HEAD, HEAD), HEAD)
            out[2 * h * HEAD : (2 * h + 1) * HEAD, :] = k_ref[0, :, at]
            out[(2 * h + 1) * HEAD : (2 * h + 2) * HEAD, :] = v_ref[0, :, at]
        out[2 * halves * HEAD :, :] = seg


def attend_kernel(stage, halves, group, levels_back, *refs):
    q_ref, s_ref, xq_ref, xs_ref = refs[:4]
    packs = refs[4 : 4 + 2 * (levels_back + 1)]
    own_out, part_out, own_sq, part_sq = refs[4 + 2 * (levels_back + 1) :]
    rows = HEAD
    width = group * HEAD
    ctx = lax.axis_index("ctx")
    side = ctx % 2
    seg_at = 2 * halves * HEAD
    own_pos, part_pos = ctx * rows, (ctx + 1 - 2 * side) * rows

    def seg_of(pack):
        return pack[seg_at : seg_at + SEG_ROWS, :].astype(jnp.float32)[:1]

    lane = lax.broadcasted_iota(jnp.int32, (rows, rows), 1)
    line = lax.broadcasted_iota(jnp.int32, (rows, rows), 0)
    bias = []
    for q_start, q_pack in ((own_pos, packs[0]), (part_pos, packs[1])):
        q_seg = turned(seg_of(q_pack))
        tiles = []
        for n, pack in enumerate(packs):
            k_start = (own_pos, part_pos)[n % 2] - (n // 2) * 2 * rows
            ok = (lane + k_start <= line + q_start) & (lane + k_start >= 0)
            ok &= q_seg == jnp.broadcast_to(seg_of(pack), (rows, rows))
            tiles.append(jnp.where(ok, 0.0, NEG))
        bias.append(jnp.concatenate(tiles, axis=1))
    bias = jnp.concatenate(bias, axis=0)
    at = 2 * stage * HEAD
    keys = jnp.concatenate([p[at : at + HEAD, :] for p in packs], axis=0)
    vals = jnp.concatenate([p[at + HEAD : at + 2 * HEAD, :] for p in packs], axis=0)
    scale = HEAD ** (-0.5) * math.log2(math.e)
    sq = [jnp.zeros((rows, HEAD), jnp.float32), jnp.zeros((rows, HEAD), jnp.float32)]
    for g in range(group):
        here = pl.ds(pl.multiple_of((side * halves + stage) * width + g * HEAD, HEAD), HEAD)
        there = slice(stage * width + g * HEAD, stage * width + (g + 1) * HEAD)
        q = jnp.concatenate([q_ref[0, :, here], xq_ref[:, there]], axis=0)
        s = lax.dot_general(q, keys, (((1,), (1,)), ((), ())), preferred_element_type=jnp.float32)
        s = s * scale + bias
        w = jnp.exp2(s - jnp.max(s, axis=1, keepdims=True))
        total = jnp.sum(w, axis=1, keepdims=True)
        att = jnp.dot(w.astype(jnp.bfloat16), vals, preferred_element_type=jnp.float32) / total
        att = att.astype(jnp.bfloat16).astype(jnp.float32)
        for n, (out, stream) in enumerate(
            ((own_out, s_ref[0, :, here]), (part_out, xs_ref[:, there]))
        ):
            adv = stream.astype(jnp.float32) + att[n * rows : (n + 1) * rows]
            adv = adv.astype(jnp.bfloat16)
            out[:, g * HEAD : (g + 1) * HEAD] = adv
            sq[n] += adv.astype(jnp.float32) ** 2
    for out, part in ((own_sq, sq[0]), (part_sq, sq[1])):
        out[...] = jnp.broadcast_to(jnp.sum(jnp.transpose(part), axis=0, keepdims=True), (8, HEAD))


def final_kernel(halves, width, *refs):
    own_parts, part_parts = refs[:halves], refs[halves : 2 * halves]
    sq_a, sq_b, gain_ref, arrived_ref, normed_ref = refs[2 * halves :]
    side = lax.axis_index("ctx") % 2
    sq = jnp.zeros((HEAD, HEAD), jnp.float32)
    for p in own_parts + part_parts:
        for g in range(width // HEAD):
            sq += p[:, g * HEAD : (g + 1) * HEAD].astype(jnp.float32) ** 2
    total = jnp.sum(jnp.transpose(sq), axis=0, keepdims=True) + sq_a[:1] + sq_b[:1]
    inv = turned(lax.rsqrt(total / FEATURES + EPS))
    for half, parts in ((side, own_parts), (1 - side, part_parts)):
        for n, p in enumerate(parts):
            for g in range(width // HEAD):
                at = pl.ds(pl.multiple_of((half * halves + n) * width + g * HEAD, HEAD), HEAD)
                a = p[:, g * HEAD : (g + 1) * HEAD]
                arrived_ref[0, :, at] = a
                gain = gain_ref[:, at].astype(jnp.float32)
                normed_ref[0, :, at] = (a.astype(jnp.float32) * inv * gain).astype(jnp.bfloat16)


def per_device(stream, queries, keys, values, segments, norm_gain):
    rows = stream.shape[1]
    kv_heads = keys.shape[2] // HEAD
    halves = kv_heads // 2
    group = queries.shape[2] // keys.shape[2]
    width = group * HEAD
    half_width = halves * width
    n_ctx = lax.axis_size("ctx")
    n_pipe = lax.axis_size("pipe")
    level = 2 * rows
    levels_back = (n_ctx * rows // 2 - 1 + level - 1) // level
    side = lax.axis_index("ctx") % 2
    pack_shape = (2 * halves * HEAD + SEG_ROWS, HEAD)
    vmem = pl.BlockSpec(memory_space=pltpu.VMEM)
    params = pltpu.CompilerParams(vmem_limit_bytes=VMEM_LIMIT)

    keep, send = pl.pallas_call(
        functools.partial(pack_kernel, halves),
        out_shape=[jax.ShapeDtypeStruct(pack_shape, jnp.bfloat16)] * 2,
        in_specs=[vmem] * 3,
        out_specs=[vmem] * 2,
        compiler_params=params,
        name="pack",
    )(keys, values, segments)

    def other(c):
        return (c + 1 - 2 * (c % 2),)

    def up(c):
        return ((c + 2) % n_ctx,)

    swapped = route(send, ["ctx"], other)
    packs = [keep, swapped]
    for _ in range(levels_back):
        packs += [route(packs[-2], ["ctx"], up), route(packs[-1], ["ctx"], up)]
    q_send = lax.dynamic_slice(queries[0], (0, (1 - side) * half_width), (rows, half_width))
    s_send = lax.dynamic_slice(stream[0], (0, (1 - side) * half_width), (rows, half_width))
    q_part = route(q_send, ["ctx"], other)
    s_part = route(s_send, ["ctx"], other)

    straight, across, own_sq, part_sq = [], [], [], []
    for stage in range(halves):
        own, part, sq_o, sq_p = pl.pallas_call(
            functools.partial(attend_kernel, stage, halves, group, levels_back),
            out_shape=[jax.ShapeDtypeStruct((rows, width), jnp.bfloat16)] * 2
            + [jax.ShapeDtypeStruct((8, HEAD), jnp.float32)] * 2,
            in_specs=[vmem] * (4 + len(packs)),
            out_specs=[vmem] * 4,
            compiler_params=params,
            name=f"attend{stage}",
        )(queries, stream, q_part, s_part, *packs)
        across.append(route(part, ["pipe", "ctx"], lambda p, c: ((p + 1) % n_pipe, *other(c))))
        straight.append(route(own, ["pipe"], lambda p: ((p + 1) % n_pipe,)))
        own_sq.append(sq_o)
        part_sq.append(sq_p)
    sq_a = route(sum(own_sq), ["pipe", "tp"], lambda p, t: ((p + 1) % n_pipe, 1 - t))
    sq_b = route(
        sum(part_sq),
        ["pipe", "ctx", "tp"],
        lambda p, c, t: ((p + 1) % n_pipe, *other(c), 1 - t),
    )
    return tuple(
        pl.pallas_call(
            functools.partial(final_kernel, halves, width),
            out_shape=[jax.ShapeDtypeStruct(stream.shape, jnp.bfloat16)] * 2,
            in_specs=[vmem] * (2 * halves + 3),
            out_specs=[vmem] * 2,
            compiler_params=params,
            name="norm",
        )(*straight, *across, sq_a, sq_b, norm_gain[None])
    )


def solution(mesh):
    spec = P("pipe", "ctx", "tp")
    return jax.shard_map(
        per_device,
        mesh=mesh,
        in_specs=(spec, spec, spec, spec, P("pipe", "ctx"), P("tp")),
        out_specs=(spec, spec),
        check_vma=False,
    )
```

```python
import functools
import math

import jax
import jax.numpy as jnp
from jax import lax
from jax.experimental import pallas as pl
from jax.experimental.pallas import tpu as pltpu
from jax.sharding import PartitionSpec as P

HEAD = 128
FEATURES = 4096
EPS = 1e-05
SEG_ROWS = 16
NEG = -1e30
VMEM_LIMIT = 40 * 1024 * 1024


def route(x, axes, move):
    sizes = [lax.axis_size(a) for a in axes]
    pairs = []
    for src in range(math.prod(sizes)):
        at, rest = [], src
        for s in reversed(sizes):
            at.insert(0, rest % s)
            rest //= s
        target = move(*at)
        if target is not None:
            to = 0
            for s, v in zip(sizes, target):
                to = to * s + v
            pairs.append((src, to))
    return lax.ppermute(x, tuple(axes) if len(axes) > 1 else axes[0], pairs)


def gate(x, *earlier):
    return pl.pallas_call(
        lambda *refs: None,
        out_shape=jax.ShapeDtypeStruct(x.shape, x.dtype),
        in_specs=[pl.BlockSpec(memory_space=pl.ANY)] * (1 + len(earlier)),
        out_specs=pl.BlockSpec(memory_space=pl.ANY),
        input_output_aliases={0: 0},
        compiler_params=pltpu.CompilerParams(vmem_limit_bytes=VMEM_LIMIT),
        name="gate",
    )(x, *earlier)


def turned(row):
    return jnp.transpose(jnp.broadcast_to(row, (HEAD, HEAD)))


class Fetches:
    def __init__(self, sems):
        self.sems, self.copies = sems, []

    def start(self, src, dst):
        self.copies.append(pltpu.make_async_copy(src, dst, self.sems.at[len(self.copies)]))
        self.copies[-1].start()

    def wait(self):
        for c in self.copies:
            c.wait()


def lanes(start, size):
    return pl.ds(pl.multiple_of(start * HEAD, HEAD), size * HEAD)


def pack_kernel(halves, tiles, k_ref, v_ref, seg_ref, q_ref, s_ref, keep, send, far, seg_buf, sems):
    side = lax.axis_index("ctx") % 2
    fetches = Fetches(sems)
    fetches.start(seg_ref, seg_buf)
    for out, half in ((keep, side), (send, 1 - side)):
        for h in range(halves):
            for n, ref in enumerate((k_ref, v_ref)):
                rows = pl.ds((2 * h + n) * HEAD, HEAD)
                fetches.start(ref.at[0, :, lanes(half * halves + h, 1)], out.at[rows])
    for n, ref in enumerate((q_ref, s_ref)):
        fetches.start(ref.at[0, :, lanes((1 - side) * tiles, tiles)], far.at[n])
    fetches.wait()
    seg = jnp.broadcast_to(seg_buf[...], (SEG_ROWS, HEAD)).astype(jnp.float32).astype(jnp.bfloat16)
    for out in (keep, send):
        out[2 * halves * HEAD :, :] = seg


def attend_kernel(own, halves, group, q_ref, s_ref, *refs):
    *packs, out, out_sq = refs
    rows = HEAD
    ctx = lax.axis_index("ctx")
    side = ctx % 2
    own_pos, part_pos = ctx * rows, (ctx + 1 - 2 * side) * rows
    seg_at = 2 * halves * HEAD

    def seg_of(pack):
        return pack[seg_at : seg_at + SEG_ROWS, :].astype(jnp.float32)[:1]

    lane = lax.broadcasted_iota(jnp.int32, (rows, rows), 1)
    line = lax.broadcasted_iota(jnp.int32, (rows, rows), 0)
    q_start, q_seg = (own_pos, packs[0]) if own else (part_pos, packs[1])
    q_seg = turned(seg_of(q_seg))
    tiles = []
    for n, pack in enumerate(packs):
        k_start = (own_pos, part_pos)[n % 2] - (n // 2) * 2 * rows
        ok = (lane + k_start <= line + q_start) & (lane + k_start >= 0)
        ok &= q_seg == jnp.broadcast_to(seg_of(pack), (rows, rows))
        tiles.append(jnp.where(ok, 0.0, NEG))
    bias = jnp.concatenate(tiles, axis=1)
    scale = HEAD ** (-0.5) * math.log2(math.e)
    sq = jnp.zeros((rows, HEAD), jnp.float32)
    for h in range(halves):
        at = 2 * h * HEAD
        keys = jnp.concatenate([p[at : at + HEAD, :] for p in packs], axis=0)
        vals = jnp.concatenate([p[at + HEAD : at + 2 * HEAD, :] for p in packs], axis=0)
        here = [h * group + g for g in range(group)]
        if own:
            q = [q_ref[0, :, lanes(side * halves * group + n, 1)] for n in here]
        else:
            q = [q_ref[0, :, n * HEAD : (n + 1) * HEAD] for n in here]
        s = lax.dot_general(
            jnp.concatenate(q, axis=0),
            keys,
            (((1,), (1,)), ((), ())),
            preferred_element_type=jnp.float32,
        )
        s = s.reshape(group, rows, -1) * scale + bias[None]
        w = jnp.exp2(s - jnp.max(s, axis=2, keepdims=True))
        total = jnp.sum(w, axis=2, keepdims=True)
        w = w.astype(jnp.bfloat16).reshape(group * rows, -1)
        att = jnp.dot(w, vals, preferred_element_type=jnp.float32).reshape(group, rows, HEAD) / total
        att = att.astype(jnp.bfloat16).astype(jnp.float32)
        for g, n in enumerate(here):
            if own:
                stream = s_ref[0, :, lanes(side * halves * group + n, 1)]
            else:
                stream = s_ref[1, :, n * HEAD : (n + 1) * HEAD]
            adv = (stream.astype(jnp.float32) + att[g]).astype(jnp.bfloat16)
            out[:, n * HEAD : (n + 1) * HEAD] = adv
            sq += adv.astype(jnp.float32) ** 2
    out_sq[...] = row_sums(sq)


def row_sums(sq):
    return jnp.broadcast_to(jnp.sum(jnp.transpose(sq), axis=0, keepdims=True), (8, HEAD))


def final_kernel(tiles, own, part, sq_a, sq_b, gain_ref, arrived_ref, normed_ref):
    side = lax.axis_index("ctx") % 2
    sq = jnp.zeros((HEAD, HEAD), jnp.float32)
    for p in (own, part):
        for n in range(tiles):
            sq += p[:, n * HEAD : (n + 1) * HEAD].astype(jnp.float32) ** 2
    total = (row_sums(sq) + sq_a[...] + sq_b[...])[:1]
    inv = turned(lax.rsqrt(total / FEATURES + EPS))
    for half, p in ((side, own), (1 - side, part)):
        for n in range(tiles):
            a = p[:, n * HEAD : (n + 1) * HEAD]
            at = lanes(half * tiles + n, 1)
            arrived_ref[0, :, at] = a
            gain = gain_ref[:, at].astype(jnp.float32)
            normed_ref[0, :, at] = (a.astype(jnp.float32) * inv * gain).astype(jnp.bfloat16)


def per_device(stream, queries, keys, values, segments, norm_gain):
    rows = stream.shape[1]
    halves = keys.shape[2] // HEAD // 2
    group = queries.shape[2] // keys.shape[2]
    tiles = halves * group
    n_ctx = lax.axis_size("ctx")
    n_pipe = lax.axis_size("pipe")
    level = 2 * rows
    levels_back = (n_ctx * rows // 2 - 1 + level - 1) // level
    vmem = pl.BlockSpec(memory_space=pltpu.VMEM)
    anywhere = pl.BlockSpec(memory_space=pl.ANY)
    params = pltpu.CompilerParams(vmem_limit_bytes=VMEM_LIMIT)
    sums = jax.ShapeDtypeStruct((8, HEAD), jnp.float32)

    def other(c):
        return c + 1 - 2 * (c % 2)

    def up(c):
        return (c + 2) % n_ctx

    def after(p):
        return (p + 1) % n_pipe

    def hop(p, c, distance):
        z, x = c // 2, c % 2
        if z < distance:
            return after(p), c
        return p, 2 * (z + 1 if 2 * z + 2 < n_ctx else distance) + x

    def buffer(*shape):
        return jax.ShapeDtypeStruct(shape, jnp.bfloat16)

    def held(x):
        return pltpu.with_memory_space_constraint(x, pltpu.HBM)

    keep, send, far = pl.pallas_call(
        functools.partial(pack_kernel, halves, tiles),
        out_shape=[buffer(2 * halves * HEAD + SEG_ROWS, HEAD)] * 2 + [buffer(2, rows, tiles * HEAD)],
        in_specs=[anywhere] * 5,
        out_specs=[vmem] * 3,
        scratch_shapes=[pltpu.VMEM((1, rows), jnp.int32), pltpu.SemaphoreType.DMA((3 + 4 * halves,))],
        compiler_params=params,
        name="pack",
    )(*(held(x) for x in (keys, values, segments, queries, stream)))
    packs = [
        keep,
        route(send, ["ctx"], lambda c: (other(c),)),
        route(keep, ["ctx"], lambda c: (up(c),)),
        route(send, ["ctx"], lambda c: (up(other(c)),)),
    ]
    far = route(gate(far, packs[1]), ["ctx"], lambda c: (other(c),))
    for n in range(1, levels_back):
        packs += [route(b, ["pipe", "ctx"], lambda p, c: hop(p, c, n)) for b in packs[-2:]]
    def attend(own, q, s):
        return pl.pallas_call(
            functools.partial(attend_kernel, own, halves, group),
            out_shape=[buffer(rows, tiles * HEAD), sums],
            in_specs=[vmem] * (2 + len(packs)),
            out_specs=[vmem] * 2,
            compiler_params=params,
            cost_estimate=pl.CostEstimate(flops=3000000000 if own else 1000000000, bytes_accessed=0, transcendentals=0),
            name="attend_own" if own else "attend_part",
        )(q, s, *packs)

    own, own_sq = attend(True, queries, stream)
    straight = route(own, ["pipe"], lambda p: (after(p),))
    sq_a = route(own_sq, ["pipe", "tp"], lambda p, t: (after(p), 1 - t))
    far = gate(far, own)
    part, part_sq = attend(False, far, far)
    across = route(part, ["pipe", "ctx"], lambda p, c: (after(p), other(c)))
    sq_b = route(part_sq, ["pipe", "ctx", "tp"], lambda p, c, t: (after(p), other(c), 1 - t))
    return tuple(
        pl.pallas_call(
            functools.partial(final_kernel, tiles),
            out_shape=[buffer(*stream.shape)] * 2,
            in_specs=[vmem] * 5,
            out_specs=[vmem] * 2,
            compiler_params=params,
            name="norm",
        )(straight, across, sq_a, sq_b, norm_gain[None])
    )


def solution(mesh):
    spec = P("pipe", "ctx", "tp")
    return jax.shard_map(
        per_device,
        mesh=mesh,
        in_specs=(spec, spec, spec, spec, P("pipe", "ctx"), P("tp")),
        out_specs=(spec, spec),
        check_vma=False,
    )
```

```python
import functools
import math

import jax
import jax.numpy as jnp
from jax import lax
from jax.experimental import pallas as pl
from jax.experimental.pallas import tpu as pltpu
from jax.sharding import PartitionSpec as P

HEAD = 128
FEATURES = 4096
EPS = 1e-05
SEG_ROWS = 16
NEG = -1e30
VMEM_LIMIT = 40 * 1024 * 1024


def route(x, axes, move):
    sizes = [lax.axis_size(a) for a in axes]
    pairs = []
    for src in range(math.prod(sizes)):
        at, rest = [], src
        for s in reversed(sizes):
            at.insert(0, rest % s)
            rest //= s
        target = move(*at)
        if target is not None:
            to = 0
            for s, v in zip(sizes, target):
                to = to * s + v
            pairs.append((src, to))
    return lax.ppermute(x, tuple(axes) if len(axes) > 1 else axes[0], pairs)


def gate(x, *earlier):
    return pl.pallas_call(
        lambda *refs: None,
        out_shape=jax.ShapeDtypeStruct(x.shape, x.dtype),
        in_specs=[pl.BlockSpec(memory_space=pl.ANY)] * (1 + len(earlier)),
        out_specs=pl.BlockSpec(memory_space=pl.ANY),
        input_output_aliases={0: 0},
        compiler_params=pltpu.CompilerParams(vmem_limit_bytes=VMEM_LIMIT),
        name="gate",
    )(x, *earlier)


def turned(row):
    return jnp.transpose(jnp.broadcast_to(row, (HEAD, HEAD)))


class Fetches:
    def __init__(self, sems):
        self.sems, self.copies = sems, []

    def start(self, src, dst):
        self.copies.append(pltpu.make_async_copy(src, dst, self.sems.at[len(self.copies)]))
        self.copies[-1].start()

    def wait(self):
        for c in self.copies:
            c.wait()


def lanes(start, size):
    return pl.ds(pl.multiple_of(start * HEAD, HEAD), size * HEAD)


def pack_kernel(halves, group, k_ref, v_ref, seg_ref, q_ref, keep, send, far, seg_buf, sems):
    side = lax.axis_index("ctx") % 2
    tiles = halves * group
    fetches = Fetches(sems)
    fetches.start(seg_ref, seg_buf)
    for out, half in ((keep, side), (send, 1 - side)):
        for h in range(halves):
            for n, ref in enumerate((k_ref, v_ref)):
                rows = pl.ds((2 * h + n) * HEAD, HEAD)
                fetches.start(ref.at[0, :, lanes(half * halves + h, 1)], out.at[rows])
    fetches.start(q_ref.at[0, :, lanes((1 - side) * tiles, tiles)], far)
    fetches.wait()
    seg = jnp.broadcast_to(seg_buf[...], (SEG_ROWS, HEAD)).astype(jnp.float32).astype(jnp.bfloat16)
    for out in (keep, send):
        out[2 * halves * HEAD :, :] = seg


def stream_kernel(tiles, s_ref, _, __, out, sems):
    side = lax.axis_index("ctx") % 2
    fetches = Fetches(sems)
    fetches.start(s_ref.at[0, :, lanes((1 - side) * tiles, tiles)], out)
    fetches.wait()


def masks(halves, own, packs, blocks):
    rows = HEAD
    ctx = lax.axis_index("ctx")
    side = ctx % 2
    starts = ctx * rows, (ctx + 1 - 2 * side) * rows
    seg_at = 2 * halves * HEAD

    def seg_of(pack):
        return pack[seg_at : seg_at + SEG_ROWS, :].astype(jnp.float32)[:1]

    lane = lax.broadcasted_iota(jnp.int32, (rows, rows), 1)
    line = lax.broadcasted_iota(jnp.int32, (rows, rows), 0)
    q_seg = turned(seg_of(own[1]))
    tiles = []
    for pack, n in zip(packs, blocks):
        k_start = starts[n % 2] - (n // 2) * 2 * rows
        ok = (lane + k_start <= line + starts[own[0]]) & (lane + k_start >= 0)
        ok &= q_seg == jnp.broadcast_to(seg_of(pack), (rows, rows))
        tiles.append(jnp.where(ok, 0.0, NEG))
    return jnp.concatenate(tiles, axis=1)


def partial_attention(h, group, q, packs, bias, top=None):
    at = 2 * h * HEAD
    keys = jnp.concatenate([p[at : at + HEAD, :] for p in packs], axis=0)
    vals = jnp.concatenate([p[at + HEAD : at + 2 * HEAD, :] for p in packs], axis=0)
    s = lax.dot_general(q, keys, (((1,), (1,)), ((), ())), preferred_element_type=jnp.float32)
    s = s.reshape(group, HEAD, -1) * (HEAD ** (-0.5) * math.log2(math.e)) + bias[None]
    tops = [s[:, :, n * HEAD : (n + 1) * HEAD] for n in range(len(packs))]
    if top is not None:
        tops.append(top)
    new_top = jnp.max(functools.reduce(jnp.maximum, tops), axis=2, keepdims=True)
    w = jnp.exp2(s - new_top)
    total = jnp.sum(w, axis=2, keepdims=True)
    w = w.astype(jnp.bfloat16).reshape(group * HEAD, -1)
    acc = jnp.dot(w, vals, preferred_element_type=jnp.float32).reshape(group, HEAD, HEAD)
    return acc, new_top, total


def own_queries(q_ref, h, halves, group):
    side = lax.axis_index("ctx") % 2
    at = [lanes((side * halves + h) * group + g, 1) for g in range(group)]
    return jnp.concatenate([q_ref[0, :, a] for a in at], axis=0)


def near_kernel(halves, group, blocks, q_ref, *refs):
    *packs, accs, tops, totals = refs
    bias = masks(halves, (0, packs[0]), packs, blocks)
    for h in range(halves):
        q = own_queries(q_ref, h, halves, group)
        acc, top, total = partial_attention(h, group, q, packs, bias)
        accs[h] = acc
        tops[h] = jnp.broadcast_to(top, acc.shape)
        totals[h] = jnp.broadcast_to(total, acc.shape)


def own_kernel(halves, group, blocks, q_ref, s_ref, accs, tops, totals, keep, *refs):
    *packs, out, out_sq = refs
    side = lax.axis_index("ctx") % 2
    bias = masks(halves, (0, keep), packs, blocks)
    sq = jnp.zeros((HEAD, HEAD), jnp.float32)
    for h in range(halves):
        q = own_queries(q_ref, h, halves, group)
        acc, top, total = partial_attention(h, group, q, packs, bias, tops[h])
        scale = jnp.exp2(tops[h] - top)
        acc = accs[h] * scale + acc
        total = totals[h] * scale + total
        att = (acc / total).astype(jnp.bfloat16).astype(jnp.float32)
        for g in range(group):
            n = h * group + g
            stream = s_ref[0, :, lanes(side * halves * group + n, 1)].astype(jnp.float32)
            adv = (stream + att[g]).astype(jnp.bfloat16)
            out[:, n * HEAD : (n + 1) * HEAD] = adv
            sq += adv.astype(jnp.float32) ** 2
    out_sq[...] = row_sums(sq)


def part_kernel(halves, group, q_ref, _, *refs):
    *packs, out = refs
    bias = masks(halves, (1, packs[1]), packs, range(len(packs)))
    for h in range(halves):
        tiles = range(h * group, (h + 1) * group)
        q = jnp.concatenate([q_ref[:, n * HEAD : (n + 1) * HEAD] for n in tiles], axis=0)
        acc, _, total = partial_attention(h, group, q, packs, bias)
        att = (acc / total).astype(jnp.bfloat16)
        for g in range(group):
            n = h * group + g
            out[:, n * HEAD : (n + 1) * HEAD] = att[g]


def add_kernel(tiles, s_ref, att_ref, out, out_sq):
    sq = jnp.zeros((HEAD, HEAD), jnp.float32)
    for n in range(tiles):
        at = slice(n * HEAD, (n + 1) * HEAD)
        adv = s_ref[:, at].astype(jnp.float32) + att_ref[:, at].astype(jnp.float32)
        adv = adv.astype(jnp.bfloat16)
        out[:, at] = adv
        sq += adv.astype(jnp.float32) ** 2
    out_sq[...] = row_sums(sq)


def row_sums(sq):
    return jnp.broadcast_to(jnp.sum(jnp.transpose(sq), axis=0, keepdims=True), (8, HEAD))


def final_kernel(tiles, own, part, sq_a, sq_b, gain_ref, arrived_ref, normed_ref, held, sems):
    side = lax.axis_index("ctx") % 2
    halves = ((side, own), (1 - side, part))
    copies = Fetches(sems)
    for half, p in halves:
        copies.start(p, arrived_ref.at[0, :, lanes(half * tiles, tiles)])
    sq = jnp.zeros((HEAD, HEAD), jnp.float32)
    for p in (own, part):
        for n in range(tiles):
            sq += p[:, n * HEAD : (n + 1) * HEAD].astype(jnp.float32) ** 2
    total = (row_sums(sq) + sq_a[...] + sq_b[...])[:1]
    inv = turned(lax.rsqrt(total / FEATURES + EPS))
    for i, (half, p) in enumerate(halves):
        for n in range(tiles):
            a = p[:, n * HEAD : (n + 1) * HEAD].astype(jnp.float32)
            gain = gain_ref[:, lanes(half * tiles + n, 1)].astype(jnp.float32)
            held[i, :, n * HEAD : (n + 1) * HEAD] = (a * inv * gain).astype(jnp.bfloat16)
        copies.start(held.at[i], normed_ref.at[0, :, lanes(half * tiles, tiles)])
    copies.wait()


def per_device(stream, queries, keys, values, segments, norm_gain):
    rows = stream.shape[1]
    halves = keys.shape[2] // HEAD // 2
    group = queries.shape[2] // keys.shape[2]
    tiles = halves * group
    n_ctx = lax.axis_size("ctx")
    n_pipe = lax.axis_size("pipe")
    level = 2 * rows
    levels_back = (n_ctx * rows // 2 - 1 + level - 1) // level
    vmem = pl.BlockSpec(memory_space=pltpu.VMEM)
    anywhere = pl.BlockSpec(memory_space=pl.ANY)
    params = pltpu.CompilerParams(vmem_limit_bytes=VMEM_LIMIT)
    sums = jax.ShapeDtypeStruct((8, HEAD), jnp.float32)

    def other(c):
        return c + 1 - 2 * (c % 2)

    def up(c):
        return (c + 2) % n_ctx

    def after(p):
        return (p + 1) % n_pipe

    def hop(p, c, distance):
        z, x = c // 2, c % 2
        if z < distance:
            return after(p), c
        return p, 2 * (z + 1 if 2 * z + 2 < n_ctx else distance) + x

    def buffer(*shape):
        return jax.ShapeDtypeStruct(shape, jnp.bfloat16)

    def held(x):
        return pltpu.with_memory_space_constraint(x, pltpu.HBM)

    def kernel(body, name, shapes, specs, *args, scratch=(), flops=0):
        return pl.pallas_call(
            body,
            out_shape=shapes,
            in_specs=specs,
            out_specs=[vmem] * len(shapes),
            scratch_shapes=scratch,
            compiler_params=params,
            cost_estimate=pl.CostEstimate(flops=flops, bytes_accessed=0, transcendentals=0),
            name=name,
        )(*args)

    kv_rows = 2 * halves * HEAD + SEG_ROWS
    keep, send, far_q = kernel(
        functools.partial(pack_kernel, halves, group),
        "pack",
        [buffer(kv_rows, HEAD)] * 2 + [buffer(rows, tiles * HEAD)],
        [anywhere] * 4,
        *(held(x) for x in (keys, values, segments, queries)),
        scratch=[pltpu.VMEM((1, rows), jnp.int32), pltpu.SemaphoreType.DMA((2 + 4 * halves,))],
    )
    packs = [
        keep,
        route(send, ["ctx"], lambda c: (other(c),)),
        route(keep, ["ctx"], lambda c: (up(c),)),
        route(send, ["ctx"], lambda c: (up(other(c)),)),
    ]
    far_q = route(gate(far_q, packs[1]), ["ctx"], lambda c: (other(c),))
    for n in range(1, levels_back):
        packs += [route(b, ["pipe", "ctx"], lambda p, c: hop(p, c, n)) for b in packs[-2:]]
    (far,) = kernel(
        functools.partial(stream_kernel, tiles),
        "stream",
        [buffer(rows, tiles * HEAD)],
        [anywhere] * 3,
        held(stream),
        packs[2],
        packs[3],
        scratch=[pltpu.SemaphoreType.DMA((1,))],
    )
    far = route(far, ["ctx"], lambda c: (other(c),))

    near, late = [0, 2, 3], [1, *range(4, len(packs))]
    state = [jax.ShapeDtypeStruct((halves, group, rows, HEAD), jnp.float32)] * 3
    state = kernel(
        functools.partial(near_kernel, halves, group, near),
        "attend_near",
        state,
        [vmem] * (1 + len(near)),
        queries,
        *(packs[n] for n in near),
        flops=1000000000,
    )
    own, own_sq = kernel(
        functools.partial(own_kernel, halves, group, late),
        "attend_own",
        [buffer(rows, tiles * HEAD), sums],
        [vmem] * (6 + len(late)),
        queries,
        stream,
        *state,
        keep,
        *(packs[n] for n in late),
        flops=1000000000,
    )
    straight = route(own, ["pipe"], lambda p: (after(p),))
    sq_a = route(own_sq, ["pipe", "tp"], lambda p, t: (after(p), 1 - t))
    (att,) = kernel(
        functools.partial(part_kernel, halves, group),
        "attend_part",
        [buffer(rows, tiles * HEAD)],
        [vmem, anywhere] + [vmem] * len(packs),
        far_q,
        own,
        *packs,
        flops=1000000000,
    )
    part, part_sq = kernel(
        functools.partial(add_kernel, tiles), "add", [buffer(rows, tiles * HEAD), sums], [vmem] * 2, far, att
    )
    across = route(part, ["pipe", "ctx"], lambda p, c: (after(p), other(c)))
    sq_b = route(part_sq, ["pipe", "ctx", "tp"], lambda p, c, t: (after(p), other(c), 1 - t))
    return tuple(
        pl.pallas_call(
            functools.partial(final_kernel, tiles),
            out_shape=[buffer(*stream.shape)] * 2,
            in_specs=[vmem] * 5,
            out_specs=[anywhere] * 2,
            scratch_shapes=[pltpu.VMEM((2, rows, tiles * HEAD), jnp.bfloat16), pltpu.SemaphoreType.DMA((4,))],
            compiler_params=params,
            name="norm",
        )(straight, across, sq_a, sq_b, norm_gain[None])
    )


def solution(mesh):
    spec = P("pipe", "ctx", "tp")
    return jax.shard_map(
        per_device,
        mesh=mesh,
        in_specs=(spec, spec, spec, spec, P("pipe", "ctx"), P("tp")),
        out_specs=(spec, spec),
        check_vma=False,
    )
```

```python
import functools
import math

import jax
import jax.numpy as jnp
from jax import lax
from jax.experimental import pallas as pl
from jax.experimental.pallas import tpu as pltpu
from jax.sharding import PartitionSpec as P

HEAD = 128
FEATURES = 4096
EPS = 1e-05
SEG_ROWS = 16
NEG = -1e30
VMEM_LIMIT = 40 * 1024 * 1024


def route(x, axes, move):
    sizes = [lax.axis_size(a) for a in axes]
    pairs = []
    for src in range(math.prod(sizes)):
        at, rest = [], src
        for s in reversed(sizes):
            at.insert(0, rest % s)
            rest //= s
        target = move(*at)
        if target is not None:
            to = 0
            for s, v in zip(sizes, target):
                to = to * s + v
            pairs.append((src, to))
    return lax.ppermute(x, tuple(axes) if len(axes) > 1 else axes[0], pairs)


def gate(x, *earlier):
    return pl.pallas_call(
        lambda *refs: None,
        out_shape=jax.ShapeDtypeStruct(x.shape, x.dtype),
        in_specs=[pl.BlockSpec(memory_space=pl.ANY)] * (1 + len(earlier)),
        out_specs=pl.BlockSpec(memory_space=pl.ANY),
        input_output_aliases={0: 0},
        compiler_params=pltpu.CompilerParams(vmem_limit_bytes=VMEM_LIMIT),
        name="gate",
    )(x, *earlier)


def turned(row):
    return jnp.transpose(jnp.broadcast_to(row, (HEAD, HEAD)))


class Fetches:
    def __init__(self, sems):
        self.sems, self.copies = sems, []

    def start(self, src, dst):
        self.copies.append(pltpu.make_async_copy(src, dst, self.sems.at[len(self.copies)]))
        self.copies[-1].start()

    def wait(self):
        for c in self.copies:
            c.wait()


def lanes(start, size):
    return pl.ds(pl.multiple_of(start * HEAD, HEAD), size * HEAD)


def pack_kernel(halves, group, k_ref, v_ref, seg_ref, q_ref, s_ref, keep, send, far_q, far_s, seg_buf, sems):
    side = lax.axis_index("ctx") % 2
    tiles = halves * group
    fetches = Fetches(sems)
    fetches.start(seg_ref, seg_buf)
    for out, half in ((keep, side), (send, 1 - side)):
        for h in range(halves):
            for n, ref in enumerate((k_ref, v_ref)):
                rows = pl.ds((2 * h + n) * HEAD, HEAD)
                fetches.start(ref.at[0, :, lanes(half * halves + h, 1)], out.at[rows])
    for ref, far in ((q_ref, far_q), (s_ref, far_s)):
        fetches.start(ref.at[0, :, lanes((1 - side) * tiles, tiles)], far)
    fetches.wait()
    seg = jnp.broadcast_to(seg_buf[...], (SEG_ROWS, HEAD)).astype(jnp.float32).astype(jnp.bfloat16)
    for out in (keep, send):
        out[2 * halves * HEAD :, :] = seg


def masks(halves, own, packs, blocks):
    rows = HEAD
    ctx = lax.axis_index("ctx")
    side = ctx % 2
    starts = ctx * rows, (ctx + 1 - 2 * side) * rows
    seg_at = 2 * halves * HEAD

    def seg_of(pack):
        return pack[seg_at : seg_at + SEG_ROWS, :].astype(jnp.float32)[:1]

    lane = lax.broadcasted_iota(jnp.int32, (rows, rows), 1)
    line = lax.broadcasted_iota(jnp.int32, (rows, rows), 0)
    q_seg = turned(seg_of(own[1]))
    tiles = []
    for pack, n in zip(packs, blocks):
        k_start = starts[n % 2] - (n // 2) * 2 * rows
        ok = (lane + k_start <= line + starts[own[0]]) & (lane + k_start >= 0)
        ok &= q_seg == jnp.broadcast_to(seg_of(pack), (rows, rows))
        tiles.append(jnp.where(ok, 0.0, NEG))
    return jnp.concatenate(tiles, axis=1)


def partial_attention(h, group, q, packs, bias, top=None):
    at = 2 * h * HEAD
    keys = jnp.concatenate([p[at : at + HEAD, :] for p in packs], axis=0)
    vals = jnp.concatenate([p[at + HEAD : at + 2 * HEAD, :] for p in packs], axis=0)
    s = lax.dot_general(q, keys, (((1,), (1,)), ((), ())), preferred_element_type=jnp.float32)
    s = s.reshape(group, HEAD, -1) * (HEAD ** (-0.5) * math.log2(math.e)) + bias[None]
    tops = [s[:, :, n * HEAD : (n + 1) * HEAD] for n in range(len(packs))]
    if top is not None:
        tops.append(top)
    new_top = jnp.max(functools.reduce(jnp.maximum, tops), axis=2, keepdims=True)
    w = jnp.exp2(s - new_top)
    total = jnp.sum(w, axis=2, keepdims=True)
    w = w.astype(jnp.bfloat16).reshape(group * HEAD, -1)
    acc = jnp.dot(w, vals, preferred_element_type=jnp.float32).reshape(group, HEAD, HEAD)
    return acc, new_top, total


def own_queries(q_ref, h, halves, group):
    side = lax.axis_index("ctx") % 2
    at = [lanes((side * halves + h) * group + g, 1) for g in range(group)]
    return jnp.concatenate([q_ref[0, :, a] for a in at], axis=0)


def near_kernel(halves, group, blocks, q_ref, *refs):
    *packs, accs, tops, totals = refs
    bias = masks(halves, (0, packs[0]), packs, blocks)
    for h in range(halves):
        q = own_queries(q_ref, h, halves, group)
        acc, top, total = partial_attention(h, group, q, packs, bias)
        accs[h] = acc
        tops[h] = jnp.broadcast_to(top, acc.shape)
        totals[h] = jnp.broadcast_to(total, acc.shape)


def has_late(blocks):
    return lax.axis_index("ctx") // 2 >= blocks[0] // 2


def own_kernel(halves, group, blocks, q_ref, s_ref, accs, tops, totals, keep, *refs):
    *packs, out, out_sq = refs
    side = lax.axis_index("ctx") % 2

    def finish(results):
        sq = jnp.zeros((HEAD, HEAD), jnp.float32)
        for h, (acc, total) in enumerate(results):
            att = (acc / total).astype(jnp.bfloat16).astype(jnp.float32)
            for g in range(group):
                n = h * group + g
                stream = s_ref[0, :, lanes(side * halves * group + n, 1)].astype(jnp.float32)
                adv = (stream + att[g]).astype(jnp.bfloat16)
                out[:, n * HEAD : (n + 1) * HEAD] = adv
                sq += adv.astype(jnp.float32) ** 2
        out_sq[...] = row_sums(sq)

    @pl.when(has_late(blocks))
    def _():
        bias = masks(halves, (0, keep), packs, blocks)
        results = []
        for h in range(halves):
            q = own_queries(q_ref, h, halves, group)
            acc, top, total = partial_attention(h, group, q, packs, bias, tops[h])
            scale = jnp.exp2(tops[h] - top)
            results.append((accs[h] * scale + acc, totals[h] * scale + total))
        finish(results)

    @pl.when(jnp.logical_not(has_late(blocks)))
    def _():
        finish([(accs[h], totals[h]) for h in range(halves)])


def part_kernel(halves, group, blocks, q_ref, _, *refs):
    *packs, out = refs

    def attend(packs):
        bias = masks(halves, (1, packs[1]), packs, range(len(packs)))
        for h in range(halves):
            tiles = range(h * group, (h + 1) * group)
            q = jnp.concatenate([q_ref[:, n * HEAD : (n + 1) * HEAD] for n in tiles], axis=0)
            acc, _, total = partial_attention(h, group, q, packs, bias)
            att = (acc / total).astype(jnp.bfloat16)
            for g in range(group):
                n = h * group + g
                out[:, n * HEAD : (n + 1) * HEAD] = att[g]

    pl.when(has_late(blocks))(lambda: attend(packs))
    pl.when(jnp.logical_not(has_late(blocks)))(lambda: attend(packs[: blocks[0]]))


def add_kernel(tiles, s_ref, att_ref, out, out_sq):
    sq = jnp.zeros((HEAD, HEAD), jnp.float32)
    for n in range(tiles):
        at = slice(n * HEAD, (n + 1) * HEAD)
        adv = s_ref[:, at].astype(jnp.float32) + att_ref[:, at].astype(jnp.float32)
        adv = adv.astype(jnp.bfloat16)
        out[:, at] = adv
        sq += adv.astype(jnp.float32) ** 2
    out_sq[...] = row_sums(sq)


def row_sums(sq):
    return jnp.broadcast_to(jnp.sum(jnp.transpose(sq), axis=0, keepdims=True), (8, HEAD))


def final_kernel(tiles, own, part, sq_a, sq_b, gain_ref, arrived_ref, normed_ref, held, sems):
    side = lax.axis_index("ctx") % 2
    halves = ((side, own), (1 - side, part))
    copies = Fetches(sems)
    for half, p in halves:
        copies.start(p, arrived_ref.at[0, :, lanes(half * tiles, tiles)])
    sq = jnp.zeros((HEAD, HEAD), jnp.float32)
    for p in (own, part):
        for n in range(tiles):
            sq += p[:, n * HEAD : (n + 1) * HEAD].astype(jnp.float32) ** 2
    total = (row_sums(sq) + sq_a[...] + sq_b[...])[:1]
    inv = turned(lax.rsqrt(total / FEATURES + EPS))
    for i, (half, p) in enumerate(halves):
        for n in range(tiles):
            a = p[:, n * HEAD : (n + 1) * HEAD].astype(jnp.float32)
            gain = gain_ref[:, lanes(half * tiles + n, 1)].astype(jnp.float32)
            held[i, :, n * HEAD : (n + 1) * HEAD] = (a * inv * gain).astype(jnp.bfloat16)
        copies.start(held.at[i], normed_ref.at[0, :, lanes(half * tiles, tiles)])
    copies.wait()


def per_device(stream, queries, keys, values, segments, norm_gain):
    rows = stream.shape[1]
    halves = keys.shape[2] // HEAD // 2
    group = queries.shape[2] // keys.shape[2]
    tiles = halves * group
    n_ctx = lax.axis_size("ctx")
    n_pipe = lax.axis_size("pipe")
    level = 2 * rows
    levels_back = (n_ctx * rows // 2 - 1 + level - 1) // level
    vmem = pl.BlockSpec(memory_space=pltpu.VMEM)
    anywhere = pl.BlockSpec(memory_space=pl.ANY)
    params = pltpu.CompilerParams(vmem_limit_bytes=VMEM_LIMIT)
    sums = jax.ShapeDtypeStruct((8, HEAD), jnp.float32)

    def other(c):
        return c + 1 - 2 * (c % 2)

    def up(c):
        return (c + 2) % n_ctx

    def after(p):
        return (p + 1) % n_pipe

    def hop(c, t, distance):
        z, x = c // 2, c % 2
        if z < distance:
            return c, 1 - t
        return 2 * (z + 1 if 2 * z + 2 < n_ctx else distance) + x, t

    def buffer(*shape):
        return jax.ShapeDtypeStruct(shape, jnp.bfloat16)

    def held(x):
        return pltpu.with_memory_space_constraint(x, pltpu.HBM)

    def kernel(body, name, shapes, specs, *args, scratch=(), flops=0):
        return pl.pallas_call(
            body,
            out_shape=shapes,
            in_specs=specs,
            out_specs=[vmem] * len(shapes),
            scratch_shapes=scratch,
            compiler_params=params,
            cost_estimate=pl.CostEstimate(flops=flops, bytes_accessed=0, transcendentals=0),
            name=name,
        )(*args)

    kv_rows = 2 * halves * HEAD + SEG_ROWS
    keep, send, far_q, far_s = kernel(
        functools.partial(pack_kernel, halves, group),
        "pack",
        [buffer(kv_rows, HEAD)] * 2 + [buffer(rows, tiles * HEAD)] * 2,
        [anywhere] * 5,
        *(held(x) for x in (keys, values, segments, queries, stream)),
        scratch=[pltpu.VMEM((1, rows), jnp.int32), pltpu.SemaphoreType.DMA((3 + 4 * halves,))],
    )
    packs = [
        keep,
        route(send, ["ctx"], lambda c: (other(c),)),
        route(keep, ["ctx"], lambda c: (up(c),)),
        route(send, ["ctx"], lambda c: (up(other(c)),)),
    ]
    far_q = route(gate(far_q, packs[1]), ["ctx"], lambda c: (other(c),))
    far_s = route(gate(far_s, packs[1]), ["ctx"], lambda c: (other(c),))
    for n in range(1, levels_back):
        packs += [route(b, ["ctx", "tp"], lambda c, t: hop(c, t, n)) for b in packs[-2:]]
    near, late = [0, 1, 2, 3], [*range(4, len(packs))]
    state = [jax.ShapeDtypeStruct((halves, group, rows, HEAD), jnp.float32)] * 3
    state = kernel(
        functools.partial(near_kernel, halves, group, near),
        "attend_near",
        state,
        [vmem] * (1 + len(near)),
        queries,
        *(packs[n] for n in near),
        flops=1000000000,
    )
    own, own_sq = kernel(
        functools.partial(own_kernel, halves, group, late),
        "attend_own",
        [buffer(rows, tiles * HEAD), sums],
        [vmem] * (6 + len(late)),
        queries,
        stream,
        *state,
        keep,
        *(packs[n] for n in late),
        flops=500000000,
    )
    straight = route(own, ["pipe"], lambda p: (after(p),))
    sq_a = route(own_sq, ["pipe", "tp"], lambda p, t: (after(p), 1 - t))
    (att,) = kernel(
        functools.partial(part_kernel, halves, group, late),
        "attend_part",
        [buffer(rows, tiles * HEAD)],
        [vmem, anywhere] + [vmem] * len(packs),
        far_q,
        own,
        *packs,
        flops=500000000,
    )
    part, part_sq = kernel(
        functools.partial(add_kernel, tiles), "add", [buffer(rows, tiles * HEAD), sums], [vmem] * 2, far_s, att
    )
    across = route(part, ["pipe", "ctx"], lambda p, c: (after(p), other(c)))
    sq_b = route(part_sq, ["pipe", "ctx", "tp"], lambda p, c, t: (after(p), other(c), 1 - t))
    return tuple(
        pl.pallas_call(
            functools.partial(final_kernel, tiles),
            out_shape=[buffer(*stream.shape)] * 2,
            in_specs=[vmem] * 5,
            out_specs=[anywhere] * 2,
            scratch_shapes=[pltpu.VMEM((2, rows, tiles * HEAD), jnp.bfloat16), pltpu.SemaphoreType.DMA((4,))],
            compiler_params=params,
            name="norm",
        )(straight, across, sq_a, sq_b, norm_gain[None])
    )


def solution(mesh):
    spec = P("pipe", "ctx", "tp")
    return jax.shard_map(
        per_device,
        mesh=mesh,
        in_specs=(spec, spec, spec, spec, P("pipe", "ctx"), P("tp")),
        out_specs=(spec, spec),
        check_vma=False,
    )
```

```python
import functools
import math

import jax
import jax.numpy as jnp
from jax import lax
from jax.experimental import pallas as pl
from jax.experimental.pallas import tpu as pltpu
from jax.sharding import PartitionSpec as P

HEAD = 128
FEATURES = 4096
EPS = 1e-05
SEG_ROWS = 16
NEG = -1e30
VMEM_LIMIT = 40 * 1024 * 1024


def route(x, axes, move):
    sizes = [lax.axis_size(a) for a in axes]
    pairs = []
    for src in range(math.prod(sizes)):
        at, rest = [], src
        for s in reversed(sizes):
            at.insert(0, rest % s)
            rest //= s
        target = move(*at)
        if target is not None:
            to = 0
            for s, v in zip(sizes, target):
                to = to * s + v
            pairs.append((src, to))
    return lax.ppermute(x, tuple(axes) if len(axes) > 1 else axes[0], pairs)


def gate(x, *earlier):
    return pl.pallas_call(
        lambda *refs: None,
        out_shape=jax.ShapeDtypeStruct(x.shape, x.dtype),
        in_specs=[pl.BlockSpec(memory_space=pl.ANY)] * (1 + len(earlier)),
        out_specs=pl.BlockSpec(memory_space=pl.ANY),
        input_output_aliases={0: 0},
        compiler_params=pltpu.CompilerParams(vmem_limit_bytes=VMEM_LIMIT),
        name="gate",
    )(x, *earlier)


def turned(row):
    return jnp.transpose(jnp.broadcast_to(row, (HEAD, HEAD)))


class Fetches:
    def __init__(self, sems):
        self.sems, self.copies = sems, []

    def start(self, src, dst):
        self.copies.append(pltpu.make_async_copy(src, dst, self.sems.at[len(self.copies)]))
        self.copies[-1].start()

    def wait(self):
        for c in self.copies:
            c.wait()


def lanes(start, size):
    return pl.ds(pl.multiple_of(start * HEAD, HEAD), size * HEAD)


def pack_kernel(halves, k_ref, v_ref, seg_ref, keep, send, seg_buf, sems):
    side = lax.axis_index("ctx") % 2
    fetches = Fetches(sems)
    fetches.start(seg_ref, seg_buf)
    for out, half in ((keep, side), (send, 1 - side)):
        for h in range(halves):
            for n, ref in enumerate((k_ref, v_ref)):
                rows = pl.ds((2 * h + n) * HEAD, HEAD)
                fetches.start(ref.at[0, :, lanes(half * halves + h, 1)], out.at[rows])
    fetches.wait()
    seg = jnp.broadcast_to(seg_buf[...], (SEG_ROWS, HEAD)).astype(jnp.float32).astype(jnp.bfloat16)
    for out in (keep, send):
        out[2 * halves * HEAD :, :] = seg


def rows_kernel(tiles, q_ref, s_ref, _, far_q, far_s, sems):
    side = lax.axis_index("ctx") % 2
    fetches = Fetches(sems)
    for ref, far in ((q_ref, far_q), (s_ref, far_s)):
        fetches.start(ref.at[0, :, lanes((1 - side) * tiles, tiles)], far)
    fetches.wait()


def masks(halves, own, packs, blocks):
    rows = HEAD
    ctx = lax.axis_index("ctx")
    side = ctx % 2
    starts = ctx * rows, (ctx + 1 - 2 * side) * rows
    seg_at = 2 * halves * HEAD

    def seg_of(pack):
        return pack[seg_at : seg_at + SEG_ROWS, :].astype(jnp.float32)[:1]

    lane = lax.broadcasted_iota(jnp.int32, (rows, rows), 1)
    line = lax.broadcasted_iota(jnp.int32, (rows, rows), 0)
    q_seg = turned(seg_of(own[1]))
    tiles = []
    for pack, n in zip(packs, blocks):
        k_start = starts[n % 2] - (n // 2) * 2 * rows
        ok = (lane + k_start <= line + starts[own[0]]) & (lane + k_start >= 0)
        ok &= q_seg == jnp.broadcast_to(seg_of(pack), (rows, rows))
        tiles.append(jnp.where(ok, 0.0, NEG))
    return jnp.concatenate(tiles, axis=1)


def partial_attention(h, group, q, packs, bias, top=None):
    at = 2 * h * HEAD
    keys = jnp.concatenate([p[at : at + HEAD, :] for p in packs], axis=0)
    vals = jnp.concatenate([p[at + HEAD : at + 2 * HEAD, :] for p in packs], axis=0)
    s = lax.dot_general(q, keys, (((1,), (1,)), ((), ())), preferred_element_type=jnp.float32)
    s = s.reshape(group, HEAD, -1) * (HEAD ** (-0.5) * math.log2(math.e)) + bias[None]
    tops = [s[:, :, n * HEAD : (n + 1) * HEAD] for n in range(len(packs))]
    if top is not None:
        tops.append(top)
    new_top = jnp.max(functools.reduce(jnp.maximum, tops), axis=2, keepdims=True)
    w = jnp.exp2(s - new_top)
    total = jnp.sum(w, axis=2, keepdims=True)
    w = w.astype(jnp.bfloat16).reshape(group * HEAD, -1)
    acc = jnp.dot(w, vals, preferred_element_type=jnp.float32).reshape(group, HEAD, HEAD)
    return acc, new_top, total


def own_queries(q_ref, h, halves, group):
    side = lax.axis_index("ctx") % 2
    at = [lanes((side * halves + h) * group + g, 1) for g in range(group)]
    return jnp.concatenate([q_ref[0, :, a] for a in at], axis=0)


def near_kernel(halves, group, blocks, q_ref, *refs):
    *packs, accs, tops, totals = refs
    bias = masks(halves, (0, packs[0]), packs, blocks)
    for h in range(halves):
        q = own_queries(q_ref, h, halves, group)
        acc, top, total = partial_attention(h, group, q, packs, bias)
        accs[h] = acc
        tops[h] = jnp.broadcast_to(top, acc.shape)
        totals[h] = jnp.broadcast_to(total, acc.shape)


def has_late(blocks):
    return lax.axis_index("ctx") // 2 >= blocks[0] // 2


def own_kernel(halves, group, blocks, q_ref, s_ref, accs, tops, totals, keep, *refs):
    *packs, out, out_sq = refs
    side = lax.axis_index("ctx") % 2

    def finish(results):
        sq = jnp.zeros((HEAD, HEAD), jnp.float32)
        for h, (acc, total) in enumerate(results):
            att = (acc / total).astype(jnp.bfloat16).astype(jnp.float32)
            for g in range(group):
                n = h * group + g
                stream = s_ref[0, :, lanes(side * halves * group + n, 1)].astype(jnp.float32)
                adv = (stream + att[g]).astype(jnp.bfloat16)
                out[:, n * HEAD : (n + 1) * HEAD] = adv
                sq += adv.astype(jnp.float32) ** 2
        out_sq[...] = row_sums(sq)

    @pl.when(has_late(blocks))
    def _():
        bias = masks(halves, (0, keep), packs, blocks)
        results = []
        for h in range(halves):
            q = own_queries(q_ref, h, halves, group)
            acc, top, total = partial_attention(h, group, q, packs, bias, tops[h])
            scale = jnp.exp2(tops[h] - top)
            results.append((accs[h] * scale + acc, totals[h] * scale + total))
        finish(results)

    @pl.when(jnp.logical_not(has_late(blocks)))
    def _():
        finish([(accs[h], totals[h]) for h in range(halves)])


def part_kernel(halves, group, blocks, q_ref, _, *refs):
    *packs, out = refs

    def attend(packs):
        bias = masks(halves, (1, packs[1]), packs, range(len(packs)))
        for h in range(halves):
            tiles = range(h * group, (h + 1) * group)
            q = jnp.concatenate([q_ref[:, n * HEAD : (n + 1) * HEAD] for n in tiles], axis=0)
            acc, _, total = partial_attention(h, group, q, packs, bias)
            att = (acc / total).astype(jnp.bfloat16)
            for g in range(group):
                n = h * group + g
                out[:, n * HEAD : (n + 1) * HEAD] = att[g]

    pl.when(has_late(blocks))(lambda: attend(packs))
    pl.when(jnp.logical_not(has_late(blocks)))(lambda: attend(packs[: blocks[0]]))


def add_kernel(tiles, s_ref, att_ref, out, out_sq):
    sq = jnp.zeros((HEAD, HEAD), jnp.float32)
    for n in range(tiles):
        at = slice(n * HEAD, (n + 1) * HEAD)
        adv = s_ref[:, at].astype(jnp.float32) + att_ref[:, at].astype(jnp.float32)
        adv = adv.astype(jnp.bfloat16)
        out[:, at] = adv
        sq += adv.astype(jnp.float32) ** 2
    out_sq[...] = row_sums(sq)


def row_sums(sq):
    return jnp.broadcast_to(jnp.sum(jnp.transpose(sq), axis=0, keepdims=True), (8, HEAD))


def final_kernel(tiles, own, part, sq_a, sq_b, gain_ref, arrived_ref, normed_ref, held, sems):
    side = lax.axis_index("ctx") % 2
    halves = ((side, own), (1 - side, part))
    copies = Fetches(sems)
    for half, p in halves:
        copies.start(p, arrived_ref.at[0, :, lanes(half * tiles, tiles)])
    sq = jnp.zeros((HEAD, HEAD), jnp.float32)
    for p in (own, part):
        for n in range(tiles):
            sq += p[:, n * HEAD : (n + 1) * HEAD].astype(jnp.float32) ** 2
    total = (row_sums(sq) + sq_a[...] + sq_b[...])[:1]
    inv = turned(lax.rsqrt(total / FEATURES + EPS))
    for i, (half, p) in enumerate(halves):
        for n in range(tiles):
            a = p[:, n * HEAD : (n + 1) * HEAD].astype(jnp.float32)
            gain = gain_ref[:, lanes(half * tiles + n, 1)].astype(jnp.float32)
            held[i, :, n * HEAD : (n + 1) * HEAD] = (a * inv * gain).astype(jnp.bfloat16)
        copies.start(held.at[i], normed_ref.at[0, :, lanes(half * tiles, tiles)])
    copies.wait()


def per_device(stream, queries, keys, values, segments, norm_gain):
    rows = stream.shape[1]
    halves = keys.shape[2] // HEAD // 2
    group = queries.shape[2] // keys.shape[2]
    tiles = halves * group
    n_ctx = lax.axis_size("ctx")
    n_pipe = lax.axis_size("pipe")
    level = 2 * rows
    levels_back = (n_ctx * rows // 2 - 1 + level - 1) // level
    vmem = pl.BlockSpec(memory_space=pltpu.VMEM)
    anywhere = pl.BlockSpec(memory_space=pl.ANY)
    params = pltpu.CompilerParams(vmem_limit_bytes=VMEM_LIMIT)
    sums = jax.ShapeDtypeStruct((8, HEAD), jnp.float32)

    def other(c):
        return c + 1 - 2 * (c % 2)

    def up(c):
        return (c + 2) % n_ctx

    def after(p):
        return (p + 1) % n_pipe

    def hop(c, t, distance):
        z, x = c // 2, c % 2
        if z < distance:
            return c, 1 - t
        return 2 * (z + 1 if 2 * z + 2 < n_ctx else distance) + x, t

    def buffer(*shape):
        return jax.ShapeDtypeStruct(shape, jnp.bfloat16)

    def held(x):
        return pltpu.with_memory_space_constraint(x, pltpu.HBM)

    def kernel(body, name, shapes, specs, *args, scratch=(), flops=0):
        return pl.pallas_call(
            body,
            out_shape=shapes,
            in_specs=specs,
            out_specs=[vmem] * len(shapes),
            scratch_shapes=scratch,
            compiler_params=params,
            cost_estimate=pl.CostEstimate(flops=flops, bytes_accessed=0, transcendentals=0),
            name=name,
        )(*args)

    kv_rows = 2 * halves * HEAD + SEG_ROWS
    keep, send = kernel(
        functools.partial(pack_kernel, halves),
        "pack",
        [buffer(kv_rows, HEAD)] * 2,
        [anywhere] * 3,
        *(held(x) for x in (keys, values, segments)),
        scratch=[pltpu.VMEM((1, rows), jnp.int32), pltpu.SemaphoreType.DMA((1 + 4 * halves,))],
    )
    packs = [
        keep,
        route(send, ["ctx"], lambda c: (other(c),)),
        route(keep, ["ctx"], lambda c: (up(c),)),
        route(send, ["ctx"], lambda c: (up(other(c)),)),
    ]
    far_q, far_s = kernel(
        functools.partial(rows_kernel, tiles),
        "rows",
        [buffer(rows, tiles * HEAD)] * 2,
        [anywhere] * 3,
        held(queries),
        held(stream),
        keep,
        scratch=[pltpu.SemaphoreType.DMA((2,))],
        flops=2000000000,
    )
    far_q = route(gate(far_q, packs[1]), ["ctx"], lambda c: (other(c),))
    far_s = route(gate(far_s, packs[1]), ["ctx"], lambda c: (other(c),))
    for n in range(1, levels_back):
        packs += [route(b, ["ctx", "tp"], lambda c, t: hop(c, t, n)) for b in packs[-2:]]
    near, late = [0, 1, 2, 3], [*range(4, len(packs))]
    state = [jax.ShapeDtypeStruct((halves, group, rows, HEAD), jnp.float32)] * 3
    state = kernel(
        functools.partial(near_kernel, halves, group, near),
        "attend_near",
        state,
        [vmem] * (1 + len(near)),
        queries,
        *(packs[n] for n in near),
        flops=1000000000,
    )
    own, own_sq = kernel(
        functools.partial(own_kernel, halves, group, late),
        "attend_own",
        [buffer(rows, tiles * HEAD), sums],
        [vmem] * (6 + len(late)),
        queries,
        stream,
        *state,
        keep,
        *(packs[n] for n in late),
        flops=500000000,
    )
    straight = route(own, ["pipe"], lambda p: (after(p),))
    sq_a = route(own_sq, ["pipe", "tp"], lambda p, t: (after(p), 1 - t))
    (att,) = kernel(
        functools.partial(part_kernel, halves, group, late),
        "attend_part",
        [buffer(rows, tiles * HEAD)],
        [vmem, anywhere] + [vmem] * len(packs),
        far_q,
        own,
        *packs,
        flops=500000000,
    )
    part, part_sq = kernel(
        functools.partial(add_kernel, tiles), "add", [buffer(rows, tiles * HEAD), sums], [vmem] * 2, far_s, att
    )
    across = route(part, ["pipe", "ctx"], lambda p, c: (after(p), other(c)))
    sq_b = route(part_sq, ["pipe", "ctx", "tp"], lambda p, c, t: (after(p), other(c), 1 - t))
    return tuple(
        pl.pallas_call(
            functools.partial(final_kernel, tiles),
            out_shape=[buffer(*stream.shape)] * 2,
            in_specs=[vmem] * 5,
            out_specs=[anywhere] * 2,
            scratch_shapes=[pltpu.VMEM((2, rows, tiles * HEAD), jnp.bfloat16), pltpu.SemaphoreType.DMA((4,))],
            compiler_params=params,
            name="norm",
        )(straight, across, sq_a, sq_b, norm_gain[None])
    )


def solution(mesh):
    spec = P("pipe", "ctx", "tp")
    return jax.shard_map(
        per_device,
        mesh=mesh,
        in_specs=(spec, spec, spec, spec, P("pipe", "ctx"), P("tp")),
        out_specs=(spec, spec),
        check_vma=False,
    )
```
